32 devices in a mesh: gx: 8 (over y, x, core), gy: 4 (over z).
Axes of the slice: x: 2, y: 2, z: 4, core: 2. Of those that a mesh axis runs over, the one named last changes fastest.
Arguments:
- inputs: bfloat16 [32, 16, 48, 512], P(('gx', 'gy')), may hold values from -6 to 6
- grad_out: bfloat16 [32, 16, 48, 512], P(('gx', 'gy')), may hold values from -6 to 6
- conv_kernel: float32 [7, 7, 512], replicated, may hold values from -0.875 to 0.875
- conv_bias: float32 [512], replicated, may hold values from -4 to 4
- layer_norm_gain: float32 [512], replicated, may hold values from 0.1 to 1.9
- layer_norm_bias: float32 [512], replicated, may hold values from -3 to 3
- w_up: bfloat16 [512, 2048], replicated, may hold values from -0.25 to 0.25
- up_bias: float32 [2048], replicated, may hold values from -3 to 3
- w_down: bfloat16 [512, 2048], replicated, may hold values from -0.125 to 0.125
- down_bias: float32 [512], replicated, may hold values from -3 to 3
- layer_scale: float32 [512], replicated, may hold values from 0.1 to 1
Outputs:
- grad_inputs: bfloat16 [32, 16, 48, 512], P(('gx', 'gy'))
- grad_kernel: float32 [7, 7, 512], replicated
- grad_conv_bias: float32 [512], replicated
- grad_ln_gain: float32 [512], replicated
- grad_ln_bias: float32 [512], replicated
- grad_w_up: float32 [512, 2048], replicated
- grad_up_bias: float32 [2048], replicated
- grad_w_down: float32 [512, 2048], replicated
- grad_down_bias: float32 [512], replicated
- grad_layer_scale: float32 [512], replicated
The draws below stay inside these ranges and needn't reach their ends.
All inputs are finite; a program needn't handle non-finite values.
Results may differ from the reference program's by a relative error of at most 0.0063.
Values sent between devices are 32-bit elements; how exact they have to be, the bound alone decides.
A program may use at most 128 MiB of HBM per device.

```python
import math
import jax
import jax.numpy as jnp
from jax import lax

C = 512
F = 2048
KS = 7
HH = 16
WW = 48
IMAGES = 32


def shard_levels(own_key, extent, pieces, low, high):
    factor_of, own = 1.0, jax.random.fold_in(own_key, 6)
    for axis_at, shards_of in pieces:
        draws = jnp.exp(jax.random.uniform(jax.random.fold_in(own, axis_at), (shards_of,), jnp.float32, low / len(pieces), high / len(pieces)))
        factor_of = factor_of * jnp.repeat(draws, extent[axis_at] // shards_of).reshape([-1 if axis == axis_at else 1 for axis in range(len(extent))])
    return factor_of


def gaussian(rng, shape, spread, reach, split=(), kind=jnp.bfloat16):
    gain = shard_levels(rng, shape, split, -0.22, 0.18) if split else 1.0
    array = jax.random.normal(rng, shape, jnp.float32) * spread * gain
    return jnp.minimum(jnp.maximum(array, -reach), reach).astype(kind)


def setup_inputs(seed: int = 0) -> dict:
    arg_keys = jax.random.split(jax.random.key(seed), 12)
    return {
        "inputs": gaussian(arg_keys[0], (IMAGES, HH, WW, C), 1.0, 6.0, ((0, 32),)),
        "grad_out": gaussian(arg_keys[1], (IMAGES, HH, WW, C), 1.0, 6.0, ((0, 32),)),
        "conv_kernel": gaussian(arg_keys[2], (KS, KS, C), (KS * KS) ** -0.5, 0.875, (), jnp.float32),
        "conv_bias": gaussian(arg_keys[3], (C,), 1.0, 4.0, (), jnp.float32),
        "layer_norm_gain": jnp.clip(1.0 + 0.18 * jax.random.normal(arg_keys[4], (C,), jnp.float32), 0.1, 1.9),
        "layer_norm_bias": gaussian(arg_keys[5], (C,), 0.5, 3.0, (), jnp.float32),
        "w_up": gaussian(arg_keys[6], (C, F), C ** -0.5, 0.25),
        "up_bias": gaussian(arg_keys[7], (F,), 0.5, 3.0, (), jnp.float32),
        "w_down": gaussian(arg_keys[8], (C, F), F ** -0.5, 0.125),
        "down_bias": gaussian(arg_keys[9], (C,), 0.5, 3.0, (), jnp.float32),
        "layer_scale": jnp.clip(jnp.exp(jax.random.uniform(arg_keys[10], (C,), jnp.float32, math.log(0.1), math.log(1.0))), 0.1, 1.0),
    }


def gelu_slope(pre):
    cdf = 0.5 * (1.0 + jax.scipy.special.erf(pre * 0.7071067811865476))
    dens = jnp.exp(-0.5 * pre * pre) * 0.3989422804014327
    return cdf + pre * dens

def one_image(image_in, upstream_in, conv_kernel, conv_bias, layer_norm_gain, layer_norm_bias, w_up, up_bias, w_down, down_bias, layer_scale):
    image = image_in.astype(jnp.float32)
    row_count, column_count, channel_count = image.shape
    padded = jnp.pad(image, ((3, 3), (3, 3), (0, 0)))
    mixed = jnp.zeros_like(image) + conv_bias
    for i in range(KS):
        for j in range(KS):
            mixed = mixed + padded[i:i + row_count, j:j + column_count] * conv_kernel[i, j]
    mean_removed = mixed - lax.optimization_barrier(jnp.mean(mixed, axis=-1, keepdims=True))
    inverse_deviation = lax.rsqrt(lax.optimization_barrier(jnp.mean(mean_removed * mean_removed, axis=-1, keepdims=True)) + 1e-06)
    standardized_input = mean_removed * inverse_deviation
    normalized_output = (standardized_input * layer_norm_gain + layer_norm_bias).astype(jnp.bfloat16).reshape(row_count * column_count, channel_count)
    pre = jnp.dot(normalized_output, w_up, preferred_element_type=jnp.float32) + up_bias
    hidden = jax.nn.gelu(pre, approximate=False).astype(jnp.bfloat16)
    branch = lax.dot_general(hidden, w_down, (((1,), (1,)), ((), ())), preferred_element_type=jnp.float32) + down_bias
    upstream = upstream_in.astype(jnp.float32).reshape(row_count * column_count, channel_count)
    g_scale = lax.optimization_barrier(jnp.sum(upstream * branch, axis=0))
    g_branch = (upstream * layer_scale).astype(jnp.bfloat16)
    gw_down = lax.dot_general(g_branch, hidden, (((0,), (0,)), ((), ())), preferred_element_type=jnp.float32)
    g_down_bias = lax.optimization_barrier(jnp.sum(g_branch.astype(jnp.float32), axis=0))
    g_hidden = jnp.dot(g_branch, w_down, preferred_element_type=jnp.float32)
    g_pre = (g_hidden * gelu_slope(pre)).astype(jnp.bfloat16)
    gw_up = lax.dot_general(normalized_output, g_pre, (((0,), (0,)), ((), ())), preferred_element_type=jnp.float32)
    g_up_bias = lax.optimization_barrier(jnp.sum(g_pre.astype(jnp.float32), axis=0))
    normalized_gradient = lax.dot_general(g_pre, w_up, (((1,), (1,)), ((), ())), preferred_element_type=jnp.float32).reshape(row_count, column_count, channel_count)
    gain_gradient = lax.optimization_barrier(jnp.sum(normalized_gradient * standardized_input, axis=(0, 1)))
    g_lnbias = lax.optimization_barrier(jnp.sum(normalized_gradient, axis=(0, 1)))
    gradient_times_normalized = normalized_gradient * layer_norm_gain
    mixed_gradient = inverse_deviation * (gradient_times_normalized - lax.optimization_barrier(jnp.mean(gradient_times_normalized, axis=-1, keepdims=True)) - standardized_input * lax.optimization_barrier(jnp.mean(gradient_times_normalized * standardized_input, axis=-1, keepdims=True)))
    g_cbias = lax.optimization_barrier(jnp.sum(mixed_gradient, axis=(0, 1)))
    kernel_terms = []
    for i in range(KS):
        for j in range(KS):
            kernel_terms.append(lax.optimization_barrier(jnp.sum(mixed_gradient * padded[i:i + row_count, j:j + column_count], axis=(0, 1))))
    g_kernel = jnp.stack(kernel_terms).reshape(KS, KS, channel_count)
    gpad = jnp.pad(mixed_gradient, ((3, 3), (3, 3), (0, 0)))
    back = upstream_in.astype(jnp.float32)
    for i in range(KS):
        for j in range(KS):
            back = back + gpad[6 - i:6 - i + row_count, 6 - j:6 - j + column_count] * conv_kernel[i, j]
    grads = (g_kernel, g_cbias, gain_gradient, g_lnbias, gw_up, g_up_bias, gw_down, g_down_bias, g_scale)
    return (back.astype(jnp.bfloat16), grads)

def reference(inputs, grad_out, conv_kernel, conv_bias, layer_norm_gain, layer_norm_bias, w_up, up_bias, w_down, down_bias, layer_scale):
    channel_count = inputs.shape[3]
    hid = w_up.shape[1]
    zero_c = jnp.zeros((channel_count,), jnp.float32)
    init = (jnp.zeros((KS, KS, channel_count), jnp.float32), zero_c, zero_c, zero_c, jnp.zeros((channel_count, hid), jnp.float32), jnp.zeros((hid,), jnp.float32), jnp.zeros((channel_count, hid), jnp.float32), zero_c, zero_c)

    def step(carry, pair):
        back, grads = one_image(pair[0], pair[1], conv_kernel, conv_bias, layer_norm_gain, layer_norm_bias, w_up, up_bias, w_down, down_bias, layer_scale)
        return (jax.tree.map(lambda a, b: a + b, carry, grads), back)
    totals, grad_inputs = lax.scan(step, init, (inputs, grad_out))
    means = jax.tree.map(lambda a: a / IMAGES, totals)
    return (grad_inputs, means[0], means[1], means[2], means[3], means[4], means[5], means[6], means[7], means[8])
```

```python
import functools

import jax
import jax.numpy as jnp
from jax import lax
from jax.experimental import pallas as pl
from jax.experimental.pallas import tpu as pltpu
from jax.sharding import PartitionSpec as P

MESH = pl.DeviceIdType.MESH
LANES = 128
MARGIN = 8
F32 = jnp.float32
BF16 = jnp.bfloat16


def fill_padded(pad, rows, columns, half, read):
    pad[...] = jnp.zeros_like(pad)

    def put(h, _):
        pad[h + half, MARGIN : MARGIN + columns, :] = read(h)
        return 0

    lax.fori_loop(0, rows, put, 0)


def fill_shifts(shifts, pad, lanes, ksize, columns):
    half = ksize // 2

    def put(r, _):
        for j in range(ksize):
            start = MARGIN - half + j
            shifts[j, r] = pad[r, start : start + columns, lanes]
        return 0

    lax.fori_loop(0, pad.shape[0], put, 0)


def block_kernel(
    rows,
    columns,
    ksize,
    x_ref,
    up_ref,
    k_ref,
    cbias_ref,
    gain_ref,
    lnb_ref,
    wup_ref,
    upb_ref,
    wdown_ref,
    downb_ref,
    scale_ref,
    gmixed_ref,
    gwup_ref,
    gwdown_ref,
    small_ref,
    pad,
    shifts,
    xhat,
    inv,
    normed,
    normed_t,
    gb,
    gb_t,
    hid,
    gpre,
    gnormed,
):
    pixels, channels = xhat.shape
    hidden_units = wup_ref.shape[1]
    half = ksize // 2
    fill_padded(pad, rows, columns, half, lambda h: x_ref[h].astype(F32))
    for cb in range(channels // LANES):
        lanes = slice(cb * LANES, (cb + 1) * LANES)
        fill_shifts(shifts, pad, lanes, ksize, columns)

        def conv_row(h, _):
            total = jnp.zeros((columns, LANES), F32) + cbias_ref[:, lanes]
            for i in range(ksize):
                for j in range(ksize):
                    tap = i * ksize + j
                    total = total + shifts[j, h + i] * k_ref[tap : tap + 1, lanes]
            xhat[pl.ds(pl.multiple_of(h * columns, 8), columns), lanes] = total
            return 0

        lax.fori_loop(0, rows, conv_row, 0)

    step = columns * 2
    gain = gain_ref[...]
    small_ref[...] = jnp.zeros_like(small_ref)

    def norm_rows(b, carry):
        sum_up, sum_gb = carry
        at = pl.ds(pl.multiple_of(b * step, 16), step)
        mixed = xhat[at, :]
        removed = mixed - jnp.mean(mixed, axis=-1, keepdims=True)
        deviation = lax.rsqrt(jnp.mean(removed * removed, axis=-1, keepdims=True) + 1e-06)
        standard = removed * deviation
        xhat[at, :] = standard
        inv[at, :] = deviation
        normed[at, :] = (standard * gain + lnb_ref[...]).astype(BF16)
        upstream = up_ref[at, :].astype(F32)
        g_branch = (upstream * scale_ref[...]).astype(BF16)
        gb[at, :] = g_branch
        sum_up = sum_up + jnp.sum(upstream, axis=0, keepdims=True)
        sum_gb = sum_gb + jnp.sum(g_branch.astype(F32), axis=0, keepdims=True)
        return sum_up, sum_gb

    zero = jnp.zeros((1, channels), F32)
    sum_up, sum_gb = lax.fori_loop(0, pixels // step, norm_rows, (zero, zero))
    normed_t[...] = jnp.transpose(normed[...].astype(F32)).astype(BF16)
    gb_t[...] = jnp.transpose(gb[...].astype(F32)).astype(BF16)
    gnormed[...] = jnp.zeros_like(gnormed)
    block = channels
    small_ref[4:5, :] = sum_gb
    tall = pixels // 3

    folded = jnp.zeros((channels, LANES), F32)
    for fb in range(hidden_units // block):
        cols = slice(fb * block, (fb + 1) * block)
        bias = upb_ref[:, cols]

        def mlp_rows(b, total):
            at = pl.ds(pl.multiple_of(b * tall, 16), tall)
            pre = jnp.dot(normed[at, :], wup_ref[:, cols], preferred_element_type=F32) + bias
            cdf = 0.5 * (1.0 + lax.erf(pre * 0.7071067811865476))
            hid[at, :] = (pre * cdf).astype(BF16)
            slope = cdf + pre * (jnp.exp(-0.5 * pre * pre) * 0.3989422804014327)
            g_hidden = jnp.dot(gb[at, :], wdown_ref[:, cols], preferred_element_type=F32)
            g = (g_hidden * slope).astype(BF16)
            gpre[at, :] = g
            gnormed[at, :] += lax.dot_general(
                g, wup_ref[:, cols], (((1,), (1,)), ((), ())), preferred_element_type=F32
            )
            return total + jnp.sum(g.astype(F32), axis=0, keepdims=True)

        total = lax.fori_loop(0, 3, mlp_rows, jnp.zeros((1, block), F32))
        small_ref[6 + fb : 7 + fb, :] = total
        gwup_ref[:, cols] = jnp.dot(normed_t[...], gpre[...], preferred_element_type=F32)
        gw = jnp.dot(gb_t[...], hid[...], preferred_element_type=F32)
        gwdown_ref[:, cols] = gw
        product = gw * wdown_ref[:, cols].astype(F32)
        for part in range(block // LANES):
            folded = folded + product[:, part * LANES : (part + 1) * LANES]

    scale_sum = jnp.sum(jnp.transpose(folded), axis=0, keepdims=True)
    small_ref[5:6, :] = scale_sum / scale_ref[...] + downb_ref[...] * sum_up

    def back_rows(b, carry):
        s_gain, s_bias, s_conv = carry
        at = pl.ds(pl.multiple_of(b * step, 16), step)
        g, standard = gnormed[at, :], xhat[at, :]
        gx = g * gain
        mean_g = jnp.mean(gx, axis=-1, keepdims=True)
        mean_gx = jnp.mean(gx * standard, axis=-1, keepdims=True)
        gm = inv[at, :] * (gx - mean_g - standard * mean_gx)
        gmixed_ref[at, :] = gm
        return (
            s_gain + jnp.sum(g * standard, axis=0, keepdims=True),
            s_bias + jnp.sum(g, axis=0, keepdims=True),
            s_conv + jnp.sum(gm, axis=0, keepdims=True),
        )

    s_gain, s_bias, s_conv = lax.fori_loop(0, pixels // step, back_rows, (zero, zero, zero))
    small_ref[1:2, :] = s_conv
    small_ref[2:3, :] = s_gain
    small_ref[3:4, :] = s_bias


def add_rows(target, at, source, source_at, count, cols):
    def one(r, _):
        to = pl.ds(pl.multiple_of(at + r * 8, 8), 8)
        here = pl.ds(pl.multiple_of(source_at + r * 8, 8), 8)
        target[to, :] += source[here, cols]
        return 0

    lax.fori_loop(0, count // 8, one, 0)


def piece_shape(size, width, parts):
    across = min(parts, width // LANES)
    return across, size * across // parts, width // across


def reduce_steps(gx_count, gy_count, order, acc, out, base, width, recv, zrecv, sends, recvs, pending):
    gi, zi = lax.axis_index("gx"), lax.axis_index("gy")
    fraction = 1.0 / (gx_count * gy_count)
    all_cols = slice(base, base + width)
    slot = [0]

    def send(src, dst, gx_to, gy_to):
        n = slot[0]
        slot[0] += 1
        copy = pltpu.make_async_remote_copy(
            src_ref=src,
            dst_ref=dst,
            send_sem=sends.at[n],
            recv_sem=recvs.at[n],
            device_id=(gx_to, gy_to),
            device_id_type=MESH,
        )
        copy.start()
        pending.append(copy)
        return copy

    def rows_at(at, n):
        return pl.ds(pl.multiple_of(at, 8), n)

    size, at, filled = acc.shape[0], 0, 0
    source, source_at, cols = acc, 0, all_cols
    for b in order:
        bit = (gi // 2**b) % 2
        other = gi + (1 - 2 * bit) * 2**b
        size //= 2
        give = source.at[rows_at(source_at + (1 - bit) * size, size), cols]
        copy = send(give, recv.at[filled : filled + size, :], other, zi)
        yield
        copy.wait_recv()
        add_rows(recv, filled, source, source_at + bit * size, size, cols)
        source, source_at, cols = recv, filled, slice(0, width)
        filled += size
        at = at + bit * size

    across, prows, pcols = piece_shape(size, width, gy_count)

    def piece(ref, z, top, left):
        there = rows_at(top + (z // across) * prows, prows)
        return ref.at[there, pl.ds(pl.multiple_of(left + (z % across) * pcols, LANES), pcols)]

    copies = []
    for d in range(1, gy_count):
        z = (zi + d) % gy_count
        copies.append(send(piece(recv, z, source_at, 0), zrecv.at[d - 1], gi, z))
    yield
    total = piece(recv, zi, source_at, 0)[...]
    for d in range(1, gy_count):
        copies[d - 1].wait_recv()
        total = total + zrecv[d - 1]
    done = piece(out, zi, at, base)
    done[...] = total * fraction
    copies = []
    for d in range(1, gy_count):
        z = (zi + d) % gy_count
        copies.append(send(done, done, gi, z))
    yield
    for copy in copies:
        copy.wait_recv()
    for b in reversed(order):
        bit = (gi // 2**b) % 2
        other = gi + (1 - 2 * bit) * 2**b
        mine = out.at[rows_at(at, size), all_cols]
        copy = send(mine, mine, other, zi)
        at = at - bit * size
        size *= 2
        yield
        copy.wait_recv()


def reduce_kernel(
    gx_count,
    gy_count,
    chunks,
    rows,
    columns,
    ksize,
    gwup_ref,
    gwdown_ref,
    small_ref,
    gm_ref,
    x_ref,
    up_ref,
    k_ref,
    back_ref,
    out_up,
    out_down,
    out_small,
    pad_x,
    pad_g,
    shift_x,
    shift_g,
    acc_small,
    recv,
    zrecv,
    recv_small,
    zrecv_small,
    sends,
    recvs,
):
    gi, zi = lax.axis_index("gx"), lax.axis_index("gy")
    half = ksize // 2
    channels = k_ref.shape[1]
    bits = (gx_count - 1).bit_length()
    barrier = pltpu.get_barrier_semaphore()
    for b in range(bits):
        bit = (gi // 2**b) % 2
        other = gi + (1 - 2 * bit) * 2**b
        pl.semaphore_signal(barrier, inc=1, device_id=(other, zi), device_id_type=MESH)
    for d in range(1, gy_count):
        z = (zi + d) % gy_count
        pl.semaphore_signal(barrier, inc=1, device_id=(gi, z), device_id_type=MESH)
    pl.semaphore_wait(barrier, bits + gy_count - 1)

    pending = []
    orders = ([0] + list(range(1, bits)), [0] + list(range(bits - 1, 0, -1)))
    width = gwup_ref.shape[1] * 2 // chunks
    steps = []
    for n in range(chunks):
        acc, out = (gwdown_ref, out_down) if n % 2 == 0 else (gwup_ref, out_up)
        steps.append(
            reduce_steps(
                gx_count, gy_count, orders[n % 2], acc, out, (n // 2) * width, width,
                recv.at[n], zrecv.at[n], sends.at[n], recvs.at[n], pending,
            )
        )
    steps.append(
        reduce_steps(
            gx_count, gy_count, orders[0], acc_small, out_small, 0, LANES,
            recv_small, zrecv_small, sends.at[chunks], recvs.at[chunks], pending,
        )
    )

    def prepare():
        fill_padded(pad_x, rows, columns, half, lambda h: x_ref[h].astype(F32))
        fill_padded(pad_g, rows, columns, half, lambda h: gm_ref[h])
        acc_small[...] = jnp.zeros_like(acc_small)

    def conv_block(cb):
        lanes = slice(cb * LANES, (cb + 1) * LANES)
        fill_shifts(shift_x, pad_x, lanes, ksize, columns)
        fill_shifts(shift_g, pad_g, lanes, ksize, columns)
        base = cb * 64
        acc_small[base + 48 : base + 64, :] = small_ref[:, lanes]

        def back_row(h, _):
            total = up_ref[h, :, lanes].astype(F32)
            for i in range(ksize):
                for j in range(ksize):
                    tap = i * ksize + j
                    total = total + (
                        shift_g[ksize - 1 - j, h + (ksize - 1 - i)] * k_ref[tap : tap + 1, lanes]
                    )
            back_ref[h, :, lanes] = total.astype(BF16)
            return 0

        lax.fori_loop(0, rows, back_row, 0)
        for j in range(ksize):

            def kernel_row(h, sums):
                g = shift_g[half, h + half]
                new = []
                for i in range(ksize):
                    p = g * shift_x[j, h + i]
                    part = p[0:8]
                    for w in range(8, columns, 8):
                        part = part + p[w : w + 8]
                    new.append(sums[i] + part)
                return tuple(new)

            zeros = tuple(jnp.zeros((8, LANES), F32) for _ in range(ksize))
            sums = lax.fori_loop(0, rows, kernel_row, zeros)
            for i in range(ksize):
                row = base + i * ksize + j
                acc_small[row : row + 1, :] = jnp.sum(sums[i], axis=0, keepdims=True)

    blocks = channels // LANES
    work = {0: [prepare]}
    for cb in range(blocks):
        work.setdefault(cb, []).append(functools.partial(conv_block, cb))
    begin = [(n // 2) * 2 for n in range(chunks)] + [blocks]
    live = list(enumerate(steps))
    tick = 0
    while live:
        left = []
        for n, step in live:
            if tick < begin[n]:
                left.append((n, step))
                continue
            try:
                next(step)
                left.append((n, step))
            except StopIteration:
                pass
        live = left
        for job in work.get(tick, []):
            job()
        tick += 1
    for copy in pending:
        copy.wait_send()


def shards(
    gx_count,
    gy_count,
    inputs,
    grad_out,
    conv_kernel,
    conv_bias,
    layer_norm_gain,
    layer_norm_bias,
    w_up,
    up_bias,
    w_down,
    down_bias,
    layer_scale,
):
    _, rows, columns, channels = inputs.shape
    ksize = conv_kernel.shape[0]
    pixels = rows * columns
    hidden_units = w_up.shape[1]
    image, upstream = inputs[0], grad_out[0]
    taps = conv_kernel.reshape(ksize * ksize, channels)
    line = lambda v: v.reshape(1, -1)
    vmem = pl.BlockSpec(memory_space=pltpu.VMEM)
    high = rows + ksize - 1
    wide = -(-(columns + 2 * MARGIN) // 8) * 8
    pad = pltpu.VMEM((high, wide, channels), F32)
    shift = pltpu.VMEM((ksize, high, columns, LANES), F32)
    limit = 58 * 1024 * 1024

    gmixed, gwup, gwdown, small = pl.pallas_call(
        functools.partial(block_kernel, rows, columns, ksize),
        out_shape=(
            jax.ShapeDtypeStruct((pixels, channels), F32),
            jax.ShapeDtypeStruct((channels, hidden_units), F32),
            jax.ShapeDtypeStruct((channels, hidden_units), F32),
            jax.ShapeDtypeStruct((16, channels), F32),
        ),
        in_specs=[vmem] * 11,
        out_specs=(vmem,) * 4,
        scratch_shapes=[
            pad,
            shift,
            pltpu.VMEM((pixels, channels), F32),
            pltpu.VMEM((pixels, 1), F32),
            pltpu.VMEM((pixels, channels), BF16),
            pltpu.VMEM((channels, pixels), BF16),
            pltpu.VMEM((pixels, channels), BF16),
            pltpu.VMEM((channels, pixels), BF16),
            pltpu.VMEM((pixels, channels), BF16),
            pltpu.VMEM((pixels, channels), BF16),
            pltpu.VMEM((pixels, channels), F32),
        ],
        compiler_params=pltpu.CompilerParams(vmem_limit_bytes=limit),
    )(
        image,
        upstream.reshape(pixels, channels),
        taps,
        line(conv_bias),
        line(layer_norm_gain),
        line(layer_norm_bias),
        w_up,
        line(up_bias),
        w_down,
        line(down_bias),
        line(layer_scale),
    )

    chunks = 4
    blocks = channels // LANES
    bits = (gx_count - 1).bit_length()
    small_rows = max(blocks * 64, 8 * gx_count * gy_count)
    width = 2 * hidden_units // chunks
    others = gy_count - 1
    slots = 2 * (bits + others)
    back, whole_up, whole_down, whole_small = pl.pallas_call(
        functools.partial(reduce_kernel, gx_count, gy_count, chunks, rows, columns, ksize),
        out_shape=(
            jax.ShapeDtypeStruct((rows, columns, channels), BF16),
            jax.ShapeDtypeStruct((channels, hidden_units), F32),
            jax.ShapeDtypeStruct((channels, hidden_units), F32),
            jax.ShapeDtypeStruct((small_rows, LANES), F32),
        ),
        in_specs=[vmem] * 7,
        out_specs=(vmem,) * 4,
        scratch_shapes=[
            pad,
            pad,
            shift,
            shift,
            pltpu.VMEM((small_rows, LANES), F32),
            pltpu.VMEM((chunks, channels, width), F32),
            pltpu.VMEM((chunks, others) + piece_shape(channels // gx_count, width, gy_count)[1:], F32),
            pltpu.VMEM((small_rows, LANES), F32),
            pltpu.VMEM((others,) + piece_shape(small_rows // gx_count, LANES, gy_count)[1:], F32),
            pltpu.SemaphoreType.DMA((chunks + 1, slots)),
            pltpu.SemaphoreType.DMA((chunks + 1, slots)),
        ],
        compiler_params=pltpu.CompilerParams(
            collective_id=0, has_side_effects=True, vmem_limit_bytes=limit
        ),
    )(gwup, gwdown, small, gmixed.reshape(rows, columns, channels), image, upstream, taps)

    table = jnp.transpose(whole_small[: blocks * 64].reshape(blocks, 64, LANES), (1, 0, 2))
    table = table.reshape(64, channels)
    count = ksize * ksize
    return (
        back[None],
        table[:count].reshape(ksize, ksize, channels),
        table[49],
        table[50],
        table[51],
        whole_up,
        table[54 : 54 + hidden_units // channels].reshape(-1),
        whole_down,
        table[52],
        table[53],
    )


def solution(mesh):
    image = P(("gx", "gy"), None, None, None)
    return jax.shard_map(
        functools.partial(shards, mesh.shape["gx"], mesh.shape["gy"]),
        mesh=mesh,
        in_specs=(image, image) + (P(),) * 9,
        out_specs=(image,) + (P(),) * 9,
        check_vma=False,
    )
```

```python
import functools

import jax
import jax.numpy as jnp
from jax import lax
from jax.experimental import pallas as pl
from jax.experimental.pallas import tpu as pltpu
from jax.sharding import PartitionSpec as P

MESH = pl.DeviceIdType.MESH
LANES = 128
MARGIN = 8
F32 = jnp.float32
BF16 = jnp.bfloat16


def fill_padded(pad, rows, columns, half, read):
    pad[...] = jnp.zeros_like(pad)

    def put(h, _):
        pad[h + half, MARGIN : MARGIN + columns, :] = read(h)
        return 0

    lax.fori_loop(0, rows, put, 0)


def fill_shifts(shifts, pad, lanes, ksize, columns):
    half = ksize // 2

    def put(r, _):
        for j in range(ksize):
            start = MARGIN - half + j
            shifts[j, r] = pad[r, start : start + columns, lanes]
        return 0

    lax.fori_loop(0, pad.shape[0], put, 0)


def add_rows(target, at, source, source_at, count, cols):
    def one(r, _):
        to = pl.ds(pl.multiple_of(at + r * 8, 8), 8)
        here = pl.ds(pl.multiple_of(source_at + r * 8, 8), 8)
        target[to, :] += source[here, cols]
        return 0

    lax.fori_loop(0, count // 8, one, 0)


def piece_shape(size, width, parts):
    across = min(parts, width // LANES)
    return across, size * across // parts, width // across


def reduce_steps(gx_count, gy_count, order, acc, out, base, width, recv, zrecv, sends, recvs, pending):
    gi, zi = lax.axis_index("gx"), lax.axis_index("gy")
    fraction = 1.0 / (gx_count * gy_count)
    all_cols = slice(base, base + width)
    slot = [0]

    def send(src, dst, gx_to, gy_to):
        n = slot[0]
        slot[0] += 1
        copy = pltpu.make_async_remote_copy(
            src_ref=src,
            dst_ref=dst,
            send_sem=sends.at[n],
            recv_sem=recvs.at[n],
            device_id=(gx_to, gy_to),
            device_id_type=MESH,
        )
        copy.start()
        pending.append(copy)
        return copy

    def rows_at(at, n):
        return pl.ds(pl.multiple_of(at, 8), n)

    size, at, filled = acc.shape[0], 0, 0
    source, source_at, cols = acc, 0, all_cols
    for b in order:
        bit = (gi // 2**b) % 2
        other = gi + (1 - 2 * bit) * 2**b
        size //= 2
        give = source.at[rows_at(source_at + (1 - bit) * size, size), cols]
        copy = send(give, recv.at[filled : filled + size, :], other, zi)
        yield
        copy.wait_recv()
        add_rows(recv, filled, source, source_at + bit * size, size, cols)
        source, source_at, cols = recv, filled, slice(0, width)
        filled += size
        at = at + bit * size

    across, prows, pcols = piece_shape(size, width, gy_count)

    def piece(ref, z, top, left):
        there = rows_at(top + (z // across) * prows, prows)
        return ref.at[there, pl.ds(pl.multiple_of(left + (z % across) * pcols, LANES), pcols)]

    copies = []
    for d in range(1, gy_count):
        z = (zi + d) % gy_count
        copies.append(send(piece(recv, z, source_at, 0), zrecv.at[d - 1], gi, z))
    yield
    total = piece(recv, zi, source_at, 0)[...]
    for d in range(1, gy_count):
        copies[d - 1].wait_recv()
        total = total + zrecv[d - 1]
    done = piece(out, zi, at, base)
    done[...] = total * fraction
    copies = []
    for d in range(1, gy_count):
        z = (zi + d) % gy_count
        copies.append(send(done, done, gi, z))
    yield
    for copy in copies:
        copy.wait_recv()
    for b in reversed(order):
        bit = (gi // 2**b) % 2
        other = gi + (1 - 2 * bit) * 2**b
        mine = out.at[rows_at(at, size), all_cols]
        copy = send(mine, mine, other, zi)
        at = at - bit * size
        size *= 2
        yield
        copy.wait_recv()


def block_kernel(
    gx_count,
    gy_count,
    rows,
    columns,
    ksize,
    x_ref,
    up_ref,
    k_ref,
    cbias_ref,
    gain_ref,
    lnb_ref,
    wup_ref,
    upb_ref,
    wdown_ref,
    downb_ref,
    scale_ref,
    back_ref,
    up_out,
    down_out,
    small_out,
    pad_x,
    pad_g,
    shifts,
    xhat,
    inv,
    normed,
    normed_t,
    gb,
    gb_t,
    hid,
    gpre,
    gnormed,
    acc_up,
    acc_down,
    acc_small,
    full_up,
    full_down,
    recv,
    zrecv,
    recv_small,
    zrecv_small,
    sends,
    recvs,
    stores,
):
    pixels, channels = xhat.shape
    hidden_units = wup_ref.shape[1]
    half = ksize // 2
    block = channels
    blocks = channels // LANES
    bits = (gx_count - 1).bit_length()
    gi, zi = lax.axis_index("gx"), lax.axis_index("gy")
    barrier = pltpu.get_barrier_semaphore()
    for b in range(bits):
        bit = (gi // 2**b) % 2
        other = gi + (1 - 2 * bit) * 2**b
        pl.semaphore_signal(barrier, inc=1, device_id=(other, zi), device_id_type=MESH)
    for d in range(1, gy_count):
        z = (zi + d) % gy_count
        pl.semaphore_signal(barrier, inc=1, device_id=(gi, z), device_id_type=MESH)

    pending, live = [], []
    orders = ([0] + list(range(1, bits)), [0] + list(range(bits - 1, 0, -1)))

    def begin(n):
        acc, full, out = (
            (acc_down, full_down, down_out) if n % 2 == 0 else (acc_up, full_up, up_out)
        )
        cols = slice((n // 2) * block, (n // 2 + 1) * block)

        def run():
            yield from reduce_steps(
                gx_count, gy_count, orders[n % 2], acc, full, cols.start, block,
                recv.at[n], zrecv.at[n], sends.at[n], recvs.at[n], pending,
            )
            copy = pltpu.make_async_copy(full.at[:, cols], out.at[:, cols], stores.at[n])
            copy.start()
            finals.append(copy)

        return run()

    finals = []

    def advance(*fresh):
        for step in list(fresh) + live:
            try:
                next(step)
            except StopIteration:
                live.remove(step)
        live.extend(fresh)

    def put_small(row, value):
        for cb in range(blocks):
            at = cb * 64 + row
            acc_small[at : at + 1, :] = value[:, cb * LANES : (cb + 1) * LANES]

    fill_padded(pad_x, rows, columns, half, lambda h: x_ref[h].astype(F32))
    pad_g[...] = jnp.zeros_like(pad_g)
    acc_small[...] = jnp.zeros_like(acc_small)
    for cb in range(blocks):
        lanes = slice(cb * LANES, (cb + 1) * LANES)
        fill_shifts(shifts, pad_x, lanes, ksize, columns)

        def conv_row(h, _):
            total = jnp.zeros((columns, LANES), F32) + cbias_ref[:, lanes]
            for i in range(ksize):
                for j in range(ksize):
                    tap = i * ksize + j
                    total = total + shifts[j, h + i] * k_ref[tap : tap + 1, lanes]
            xhat[pl.ds(pl.multiple_of(h * columns, 8), columns), lanes] = total
            return 0

        lax.fori_loop(0, rows, conv_row, 0)

    step = columns * 2
    gain = gain_ref[...]

    def norm_rows(b, carry):
        sum_up, sum_gb = carry
        at = pl.ds(pl.multiple_of(b * step, 16), step)
        mixed = xhat[at, :]
        removed = mixed - jnp.mean(mixed, axis=-1, keepdims=True)
        deviation = lax.rsqrt(jnp.mean(removed * removed, axis=-1, keepdims=True) + 1e-06)
        standard = removed * deviation
        xhat[at, :] = standard
        inv[at, :] = deviation
        normed[at, :] = (standard * gain + lnb_ref[...]).astype(BF16)
        upstream = up_ref[at, :].astype(F32)
        g_branch = (upstream * scale_ref[...]).astype(BF16)
        gb[at, :] = g_branch
        sum_up = sum_up + jnp.sum(upstream, axis=0, keepdims=True)
        sum_gb = sum_gb + jnp.sum(g_branch.astype(F32), axis=0, keepdims=True)
        return sum_up, sum_gb

    zero = jnp.zeros((1, channels), F32)
    sum_up, sum_gb = lax.fori_loop(0, pixels // step, norm_rows, (zero, zero))
    normed_t[...] = jnp.transpose(normed[...].astype(F32)).astype(BF16)
    gb_t[...] = jnp.transpose(gb[...].astype(F32)).astype(BF16)
    gnormed[...] = jnp.zeros_like(gnormed)
    put_small(52, sum_gb)
    tall = pixels // 3

    folded = jnp.zeros((channels, LANES), F32)
    for fb in range(hidden_units // block):
        cols = slice(fb * block, (fb + 1) * block)
        bias = upb_ref[:, cols]

        def mlp_rows(b, total):
            at = pl.ds(pl.multiple_of(b * tall, 16), tall)
            pre = jnp.dot(normed[at, :], wup_ref[:, cols], preferred_element_type=F32) + bias
            cdf = 0.5 * (1.0 + lax.erf(pre * 0.7071067811865476))
            hid[at, :] = (pre * cdf).astype(BF16)
            slope = cdf + pre * (jnp.exp(-0.5 * pre * pre) * 0.3989422804014327)
            g_hidden = jnp.dot(gb[at, :], wdown_ref[:, cols], preferred_element_type=F32)
            g = (g_hidden * slope).astype(BF16)
            gpre[at, :] = g
            gnormed[at, :] += lax.dot_general(
                g, wup_ref[:, cols], (((1,), (1,)), ((), ())), preferred_element_type=F32
            )
            return total + jnp.sum(g.astype(F32), axis=0, keepdims=True)

        total = lax.fori_loop(0, 3, mlp_rows, jnp.zeros((1, block), F32))
        put_small(54 + fb, total)
        acc_up[:, cols] = jnp.dot(normed_t[...], gpre[...], preferred_element_type=F32)
        gw = jnp.dot(gb_t[...], hid[...], preferred_element_type=F32)
        acc_down[:, cols] = gw
        if fb == 0:
            pl.semaphore_wait(barrier, bits + gy_count - 1)
        advance(begin(2 * fb), begin(2 * fb + 1))
        product = gw * wdown_ref[:, cols].astype(F32)
        for part in range(block // LANES):
            folded = folded + product[:, part * LANES : (part + 1) * LANES]

    scale_sum = jnp.sum(jnp.transpose(folded), axis=0, keepdims=True)
    put_small(53, scale_sum / scale_ref[...] + downb_ref[...] * sum_up)

    def back_rows(h, carry):
        s_gain, s_bias, s_conv = carry
        at = pl.ds(pl.multiple_of(h * columns, 16), columns)
        g, standard = gnormed[at, :], xhat[at, :]
        gx = g * gain
        mean_g = jnp.mean(gx, axis=-1, keepdims=True)
        mean_gx = jnp.mean(gx * standard, axis=-1, keepdims=True)
        gm = inv[at, :] * (gx - mean_g - standard * mean_gx)
        pad_g[h + half, MARGIN : MARGIN + columns, :] = gm
        return (
            s_gain + jnp.sum(g * standard, axis=0, keepdims=True),
            s_bias + jnp.sum(g, axis=0, keepdims=True),
            s_conv + jnp.sum(gm, axis=0, keepdims=True),
        )

    s_gain, s_bias, s_conv = lax.fori_loop(0, rows, back_rows, (zero, zero, zero))
    put_small(49, s_conv)
    put_small(50, s_gain)
    put_small(51, s_bias)
    advance()

    for cb in range(blocks):
        lanes = slice(cb * LANES, (cb + 1) * LANES)
        base = cb * 64
        fill_shifts(shifts, pad_x, lanes, ksize, columns)
        for j in range(ksize):

            def kernel_row(h, sums):
                g = pad_g[h + half, MARGIN : MARGIN + columns, lanes]
                new = []
                for i in range(ksize):
                    p = g * shifts[j, h + i]
                    part = p[0:8]
                    for w in range(8, columns, 8):
                        part = part + p[w : w + 8]
                    new.append(sums[i] + part)
                return tuple(new)

            zeros = tuple(jnp.zeros((8, LANES), F32) for _ in range(ksize))
            sums = lax.fori_loop(0, rows, kernel_row, zeros)
            for i in range(ksize):
                row = base + i * ksize + j
                acc_small[row : row + 1, :] = jnp.sum(sums[i], axis=0, keepdims=True)
        if cb == blocks - 1:
            advance(
                reduce_steps(
                    gx_count, gy_count, orders[0], acc_small, small_out, 0, LANES,
                    recv_small, zrecv_small, sends.at[sends.shape[0] - 1],
                    recvs.at[recvs.shape[0] - 1], pending,
                )
            )
        elif cb % 2 == 1:
            advance()

    for cb in range(blocks):
        lanes = slice(cb * LANES, (cb + 1) * LANES)
        fill_shifts(shifts, pad_g, lanes, ksize, columns)

        def back_row(h, _):
            at = pl.ds(pl.multiple_of(h * columns, 16), columns)
            total = up_ref[at, lanes].astype(F32)
            for i in range(ksize):
                for j in range(ksize):
                    tap = i * ksize + j
                    total = total + (
                        shifts[ksize - 1 - j, h + (ksize - 1 - i)] * k_ref[tap : tap + 1, lanes]
                    )
            back_ref[at, lanes] = total.astype(BF16)
            return 0

        lax.fori_loop(0, rows, back_row, 0)
        advance()

    while live:
        advance()
    for copy in pending:
        copy.wait_send()
    for copy in finals:
        copy.wait()


def finish_kernel(
    ksize,
    up_ref,
    down_ref,
    back_ref,
    small_ref,
    back_out,
    kernel_out,
    cbias_out,
    gain_out,
    lnb_out,
    up_out,
    upb_out,
    down_out,
    downb_out,
    scale_out,
    sems,
):
    parts = 4
    tall = up_ref.shape[0] // parts
    copies = [pltpu.make_async_copy(back_ref, back_out, sems.at[2 * parts])]
    for n in range(parts):
        at = slice(n * tall, (n + 1) * tall)
        copies.append(pltpu.make_async_copy(up_ref.at[at], up_out.at[at], sems.at[2 * n]))
        copies.append(pltpu.make_async_copy(down_ref.at[at], down_out.at[at], sems.at[2 * n + 1]))
    for copy in copies:
        copy.start()
    channels = up_ref.shape[0]
    for cb in range(channels // LANES):
        base, lanes = cb * 64, slice(cb * LANES, (cb + 1) * LANES)
        for i in range(ksize):
            row = base + i * ksize
            kernel_out[i, :, lanes] = small_ref[row : row + ksize, :]
        for n, out in enumerate((cbias_out, gain_out, lnb_out, downb_out, scale_out)):
            out[:, lanes] = small_ref[base + 49 + n : base + 50 + n, :]
        for fb in range(up_ref.shape[1] // channels):
            to = fb * channels + cb * LANES
            upb_out[:, to : to + LANES] = small_ref[base + 54 + fb : base + 55 + fb, :]
    for copy in copies:
        copy.wait()


def shards(
    gx_count,
    gy_count,
    inputs,
    grad_out,
    conv_kernel,
    conv_bias,
    layer_norm_gain,
    layer_norm_bias,
    w_up,
    up_bias,
    w_down,
    down_bias,
    layer_scale,
):
    _, rows, columns, channels = inputs.shape
    ksize = conv_kernel.shape[0]
    pixels = rows * columns
    hidden_units = w_up.shape[1]
    taps = conv_kernel.reshape(ksize * ksize, channels)
    line = lambda v: v.reshape(1, -1)
    vmem = pl.BlockSpec(memory_space=pltpu.VMEM)
    anywhere = pl.BlockSpec(memory_space=pl.ANY)
    high = rows + ksize - 1
    wide = -(-(columns + 2 * MARGIN) // 8) * 8
    limit = 60 * 1024 * 1024
    blocks = channels // LANES
    bits = (gx_count - 1).bit_length()
    small_rows = max(blocks * 64, 8 * gx_count * gy_count)
    chunks = 2 * hidden_units // channels
    others = gy_count - 1
    slots = 2 * (bits + others)
    left = channels // gx_count
    weight = jax.ShapeDtypeStruct((channels, hidden_units), F32)
    wide_rows = pltpu.VMEM((pixels, channels), F32)
    narrow_rows = pltpu.VMEM((pixels, channels), BF16)
    turned_rows = pltpu.VMEM((channels, pixels), BF16)
    whole = pltpu.VMEM((channels, hidden_units), F32)
    back, whole_up, whole_down, whole_small = pl.pallas_call(
        functools.partial(block_kernel, gx_count, gy_count, rows, columns, ksize),
        out_shape=(
            jax.ShapeDtypeStruct((pixels, channels), BF16),
            weight,
            weight,
            jax.ShapeDtypeStruct((small_rows, LANES), F32),
        ),
        in_specs=[vmem] * 11,
        out_specs=(vmem, anywhere, anywhere, vmem),
        scratch_shapes=[
            pltpu.VMEM((high, wide, channels), F32),
            pltpu.VMEM((high, wide, channels), F32),
            pltpu.VMEM((ksize, high, columns, LANES), F32),
            wide_rows,
            pltpu.VMEM((pixels, 1), F32),
            narrow_rows,
            turned_rows,
            narrow_rows,
            turned_rows,
            narrow_rows,
            narrow_rows,
            wide_rows,
            whole,
            whole,
            pltpu.VMEM((small_rows, LANES), F32),
            whole,
            whole,
            pltpu.VMEM((chunks, channels - left, channels), F32),
            pltpu.VMEM((chunks, others) + piece_shape(left, channels, gy_count)[1:], F32),
            pltpu.VMEM((small_rows, LANES), F32),
            pltpu.VMEM((others,) + piece_shape(small_rows // gx_count, LANES, gy_count)[1:], F32),
            pltpu.SemaphoreType.DMA((chunks + 1, slots)),
            pltpu.SemaphoreType.DMA((chunks + 1, slots)),
            pltpu.SemaphoreType.DMA((chunks,)),
        ],
        compiler_params=pltpu.CompilerParams(
            collective_id=0, has_side_effects=True, vmem_limit_bytes=limit
        ),
    )(
        inputs[0],
        grad_out.reshape(pixels, channels),
        taps,
        line(conv_bias),
        line(layer_norm_gain),
        line(layer_norm_bias),
        w_up,
        line(up_bias),
        w_down,
        line(down_bias),
        line(layer_scale),
    )

    one = jax.ShapeDtypeStruct((1, channels), F32)
    results = pl.pallas_call(
        functools.partial(finish_kernel, ksize),
        out_shape=(
            jax.ShapeDtypeStruct((pixels, channels), BF16),
            jax.ShapeDtypeStruct(conv_kernel.shape, F32),
            one,
            one,
            one,
            weight,
            jax.ShapeDtypeStruct((1, hidden_units), F32),
            weight,
            one,
            one,
        ),
        in_specs=[anywhere, anywhere, anywhere, vmem],
        out_specs=(anywhere, vmem, vmem, vmem, vmem, anywhere, vmem, anywhere, vmem, vmem),
        scratch_shapes=[pltpu.SemaphoreType.DMA((9,))],
        compiler_params=pltpu.CompilerParams(vmem_limit_bytes=limit),
    )(whole_up, whole_down, back, whole_small)
    grad_inputs, g_kernel, cbias, ln_gain, lnb, g_up, upb, g_down, downb, scale = results
    flat = lambda v: v.reshape(-1)
    return (
        grad_inputs.reshape(inputs.shape),
        g_kernel,
        flat(cbias),
        flat(ln_gain),
        flat(lnb),
        g_up,
        flat(upb),
        g_down,
        flat(downb),
        flat(scale),
    )


def solution(mesh):
    image = P(("gx", "gy"), None, None, None)
    return jax.shard_map(
        functools.partial(shards, mesh.shape["gx"], mesh.shape["gy"]),
        mesh=mesh,
        in_specs=(image, image) + (P(),) * 9,
        out_specs=(image,) + (P(),) * 9,
        check_vma=False,
    )
```

```python
import functools

import jax
import jax.numpy as jnp
from jax import lax
from jax.experimental import pallas as pl
from jax.experimental.pallas import tpu as pltpu
from jax.sharding import PartitionSpec as P

MESH = pl.DeviceIdType.MESH
LANES = 128
MARGIN = 8
F32 = jnp.float32
BF16 = jnp.bfloat16


def fill_padded(pad, rows, columns, half, read):
    pad[...] = jnp.zeros_like(pad)

    def put(h, _):
        pad[h + half, MARGIN : MARGIN + columns, :] = read(h)
        return 0

    lax.fori_loop(0, rows, put, 0)


def fill_shifts(shifts, pad, lanes, ksize, columns):
    half = ksize // 2

    def put(r, _):
        for j in range(ksize):
            start = MARGIN - half + j
            shifts[j, r] = pad[r, start : start + columns, lanes]
        return 0

    lax.fori_loop(0, pad.shape[0], put, 0)


def add_rows(target, at, source, source_at, count, cols):
    def one(r, _):
        to = pl.ds(pl.multiple_of(at + r * 8, 8), 8)
        here = pl.ds(pl.multiple_of(source_at + r * 8, 8), 8)
        target[to, :] += source[here, cols]
        return 0

    lax.fori_loop(0, count // 8, one, 0)


def piece_shape(size, width, parts):
    across = min(parts, width // LANES)
    return across, size * across // parts, width // across


def reduce_steps(gx_count, gy_count, order, acc, out, base, width, recv, zrecv, sends, recvs, pending):
    gi, zi = lax.axis_index("gx"), lax.axis_index("gy")
    fraction = 1.0 / (gx_count * gy_count)
    all_cols = slice(base, base + width)
    slot = [0]

    def send(src, dst, gx_to, gy_to):
        n = slot[0]
        slot[0] += 1
        copy = pltpu.make_async_remote_copy(
            src_ref=src,
            dst_ref=dst,
            send_sem=sends.at[n],
            recv_sem=recvs.at[n],
            device_id=(gx_to, gy_to),
            device_id_type=MESH,
        )
        copy.start()
        pending.append(copy)
        return copy

    def rows_at(at, n):
        return pl.ds(pl.multiple_of(at, 8), n)

    size, at, filled = acc.shape[0], 0, 0
    source, source_at, cols = acc, 0, all_cols
    for b in order:
        bit = (gi // 2**b) % 2
        other = gi + (1 - 2 * bit) * 2**b
        size //= 2
        give = source.at[rows_at(source_at + (1 - bit) * size, size), cols]
        copy = send(give, recv.at[filled : filled + size, :], other, zi)
        yield
        copy.wait_recv()
        add_rows(recv, filled, source, source_at + bit * size, size, cols)
        source, source_at, cols = recv, filled, slice(0, width)
        filled += size
        at = at + bit * size

    across, prows, pcols = piece_shape(size, width, gy_count)

    def piece(ref, z, top, left):
        there = rows_at(top + (z // across) * prows, prows)
        return ref.at[there, pl.ds(pl.multiple_of(left + (z % across) * pcols, LANES), pcols)]

    copies = []
    for d in range(1, gy_count):
        z = (zi + d) % gy_count
        copies.append(send(piece(recv, z, source_at, 0), zrecv.at[d - 1], gi, z))
    yield
    total = piece(recv, zi, source_at, 0)[...]
    for d in range(1, gy_count):
        copies[d - 1].wait_recv()
        total = total + zrecv[d - 1]
    done = piece(out, zi, at, base)
    done[...] = total * fraction
    copies = []
    for d in range(1, gy_count):
        z = (zi + d) % gy_count
        copies.append(send(done, done, gi, z))
    yield
    for copy in copies:
        copy.wait_recv()
    for b in reversed(order):
        bit = (gi // 2**b) % 2
        other = gi + (1 - 2 * bit) * 2**b
        mine = out.at[rows_at(at, size), all_cols]
        copy = send(mine, mine, other, zi)
        at = at - bit * size
        size *= 2
        yield
        copy.wait_recv()


def block_kernel(
    gx_count,
    gy_count,
    rows,
    columns,
    ksize,
    x_ref,
    up_ref,
    k_ref,
    cbias_ref,
    gain_ref,
    lnb_ref,
    wup_ref,
    upb_ref,
    wdown_ref,
    downb_ref,
    scale_ref,
    back_ref,
    up_out,
    down_out,
    small_out,
    pad_x,
    pad_g,
    shifts,
    xhat,
    inv,
    normed,
    normed_t,
    gb,
    gb_t,
    hid,
    gpre,
    gnormed,
    acc_up,
    acc_down,
    acc_small,
    full_up,
    full_down,
    recv,
    zrecv,
    recv_small,
    zrecv_small,
    sends,
    recvs,
    stores,
):
    pixels, channels = xhat.shape
    hidden_units = wup_ref.shape[1]
    half = ksize // 2
    block = channels
    blocks = channels // LANES
    bits = (gx_count - 1).bit_length()
    gi, zi = lax.axis_index("gx"), lax.axis_index("gy")
    barrier = pltpu.get_barrier_semaphore()
    for b in range(bits):
        bit = (gi // 2**b) % 2
        other = gi + (1 - 2 * bit) * 2**b
        pl.semaphore_signal(barrier, inc=1, device_id=(other, zi), device_id_type=MESH)
    for d in range(1, gy_count):
        z = (zi + d) % gy_count
        pl.semaphore_signal(barrier, inc=1, device_id=(gi, z), device_id_type=MESH)

    pending, live = [], []
    orders = ([0] + list(range(1, bits)), [0] + list(range(bits - 1, 0, -1)))

    def begin(n):
        acc, full, out = (
            (acc_down, full_down, down_out) if n % 2 == 0 else (acc_up, full_up, up_out)
        )
        cols = slice((n // 2) * block, (n // 2 + 1) * block)

        def run():
            yield from reduce_steps(
                gx_count, gy_count, orders[n % 2], acc, full, cols.start, block,
                recv.at[n], zrecv.at[n], sends.at[n], recvs.at[n], pending,
            )
            copy = pltpu.make_async_copy(full.at[:, cols], out.at[:, cols], stores.at[n])
            copy.start()
            finals.append(copy)

        return run()

    finals = []

    def advance(*fresh):
        for step in list(fresh) + live:
            try:
                next(step)
            except StopIteration:
                live.remove(step)
        live[:0] = fresh

    def put_small(row, value):
        for cb in range(blocks):
            at = cb * 64 + row
            acc_small[at : at + 1, :] = value[:, cb * LANES : (cb + 1) * LANES]

    fill_padded(pad_x, rows, columns, half, lambda h: x_ref[h].astype(F32))
    pad_g[...] = jnp.zeros_like(pad_g)
    acc_small[...] = jnp.zeros_like(acc_small)
    for cb in range(blocks):
        lanes = slice(cb * LANES, (cb + 1) * LANES)
        fill_shifts(shifts, pad_x, lanes, ksize, columns)

        def conv_row(h, _):
            total = jnp.zeros((columns, LANES), F32) + cbias_ref[:, lanes]
            for i in range(ksize):
                for j in range(ksize):
                    total = total + shifts[j, h + i] * k_ref[i, j : j + 1, lanes]
            xhat[pl.ds(pl.multiple_of(h * columns, 8), columns), lanes] = total
            return 0

        lax.fori_loop(0, rows, conv_row, 0)

    step = columns * 2
    gain = gain_ref[...]

    def norm_rows(b, carry):
        sum_up, sum_gb = carry
        at = pl.ds(pl.multiple_of(b * step, 16), step)
        mixed = xhat[at, :]
        removed = mixed - jnp.mean(mixed, axis=-1, keepdims=True)
        deviation = lax.rsqrt(jnp.mean(removed * removed, axis=-1, keepdims=True) + 1e-06)
        standard = removed * deviation
        xhat[at, :] = standard
        inv[at, :] = deviation
        normed[at, :] = (standard * gain + lnb_ref[...]).astype(BF16)
        upstream = up_ref[at, :].astype(F32)
        g_branch = (upstream * scale_ref[...]).astype(BF16)
        gb[at, :] = g_branch
        sum_up = sum_up + jnp.sum(upstream, axis=0, keepdims=True)
        sum_gb = sum_gb + jnp.sum(g_branch.astype(F32), axis=0, keepdims=True)
        return sum_up, sum_gb

    zero = jnp.zeros((1, channels), F32)
    sum_up, sum_gb = lax.fori_loop(0, pixels // step, norm_rows, (zero, zero))
    normed_t[...] = jnp.transpose(normed[...].astype(F32)).astype(BF16)
    gb_t[...] = jnp.transpose(gb[...].astype(F32)).astype(BF16)
    gnormed[...] = jnp.zeros_like(gnormed)
    put_small(52, sum_gb)
    tall = pixels // 3

    folded = jnp.zeros((channels, LANES), F32)
    for fb in range(hidden_units // block):
        cols = slice(fb * block, (fb + 1) * block)
        bias = upb_ref[:, cols]

        def mlp_rows(b, total):
            at = pl.ds(pl.multiple_of(b * tall, 16), tall)
            pre = jnp.dot(normed[at, :], wup_ref[:, cols], preferred_element_type=F32) + bias
            cdf = 0.5 * (1.0 + lax.erf(pre * 0.7071067811865476))
            hid[at, :] = (pre * cdf).astype(BF16)
            slope = cdf + pre * (jnp.exp(-0.5 * pre * pre) * 0.3989422804014327)
            g_hidden = jnp.dot(gb[at, :], wdown_ref[:, cols], preferred_element_type=F32)
            g = (g_hidden * slope).astype(BF16)
            gpre[at, :] = g
            gnormed[at, :] += lax.dot_general(
                g, wup_ref[:, cols], (((1,), (1,)), ((), ())), preferred_element_type=F32
            )
            return total + jnp.sum(g.astype(F32), axis=0, keepdims=True)

        total = lax.fori_loop(0, 3, mlp_rows, jnp.zeros((1, block), F32))
        put_small(54 + fb, total)
        acc_up[:, cols] = jnp.dot(normed_t[...], gpre[...], preferred_element_type=F32)
        gw = jnp.dot(gb_t[...], hid[...], preferred_element_type=F32)
        acc_down[:, cols] = gw
        if fb == 0:
            pl.semaphore_wait(barrier, bits + gy_count - 1)
        advance(begin(2 * fb), begin(2 * fb + 1))
        product = gw * wdown_ref[:, cols].astype(F32)
        for part in range(block // LANES):
            folded = folded + product[:, part * LANES : (part + 1) * LANES]

    scale_sum = jnp.sum(jnp.transpose(folded), axis=0, keepdims=True)
    put_small(53, scale_sum / scale_ref[...] + downb_ref[...] * sum_up)

    def back_rows(h, carry):
        s_gain, s_bias, s_conv = carry
        at = pl.ds(pl.multiple_of(h * columns, 16), columns)
        g, standard = gnormed[at, :], xhat[at, :]
        gx = g * gain
        mean_g = jnp.mean(gx, axis=-1, keepdims=True)
        mean_gx = jnp.mean(gx * standard, axis=-1, keepdims=True)
        gm = inv[at, :] * (gx - mean_g - standard * mean_gx)
        pad_g[h + half, MARGIN : MARGIN + columns, :] = gm
        return (
            s_gain + jnp.sum(g * standard, axis=0, keepdims=True),
            s_bias + jnp.sum(g, axis=0, keepdims=True),
            s_conv + jnp.sum(gm, axis=0, keepdims=True),
        )

    s_gain, s_bias, s_conv = lax.fori_loop(0, rows, back_rows, (zero, zero, zero))
    put_small(49, s_conv)
    put_small(50, s_gain)
    put_small(51, s_bias)

    for cb in range(blocks):
        lanes = slice(cb * LANES, (cb + 1) * LANES)
        base = cb * 64
        fill_shifts(shifts, pad_x, lanes, ksize, columns)
        for j in range(ksize):

            def kernel_row(h, sums):
                g = pad_g[h + half, MARGIN : MARGIN + columns, lanes]
                new = []
                for i in range(ksize):
                    p = g * shifts[j, h + i]
                    part = p[0:8]
                    for w in range(8, columns, 8):
                        part = part + p[w : w + 8]
                    new.append(sums[i] + part)
                return tuple(new)

            zeros = tuple(jnp.zeros((8, LANES), F32) for _ in range(ksize))
            sums = lax.fori_loop(0, rows, kernel_row, zeros)
            for i in range(ksize):
                row = base + i * ksize + j
                acc_small[row : row + 1, :] = jnp.sum(sums[i], axis=0, keepdims=True)
        if cb == blocks - 1:
            advance(
                reduce_steps(
                    gx_count, gy_count, orders[0], acc_small, small_out, 0, LANES,
                    recv_small, zrecv_small, sends.at[sends.shape[0] - 1],
                    recvs.at[recvs.shape[0] - 1], pending,
                )
            )
        elif cb % 2 == 1:
            advance()

    for cb in range(blocks):
        lanes = slice(cb * LANES, (cb + 1) * LANES)
        fill_shifts(shifts, pad_g, lanes, ksize, columns)

        def back_row(h, _):
            at = pl.ds(pl.multiple_of(h * columns, 16), columns)
            total = up_ref[at, lanes].astype(F32)
            for i in range(ksize):
                for j in range(ksize):
                    total = total + (
                        shifts[ksize - 1 - j, h + (ksize - 1 - i)] * k_ref[i, j : j + 1, lanes]
                    )
            back_ref[at, lanes] = total.astype(BF16)
            return 0

        lax.fori_loop(0, rows, back_row, 0)
        advance()

    while live:
        advance()
    for copy in pending:
        copy.wait_send()
    for copy in finals:
        copy.wait()


def finish_kernel(
    ksize,
    up_ref,
    down_ref,
    back_ref,
    small_ref,
    back_out,
    kernel_out,
    cbias_out,
    gain_out,
    lnb_out,
    up_out,
    upb_out,
    down_out,
    downb_out,
    scale_out,
    up_hold,
    down_hold,
    back_hold,
    sems,
):
    parts = up_hold.shape[0]
    tall = up_ref.shape[0] // parts
    pairs = []
    for n in range(parts):
        at = slice(n * tall, (n + 1) * tall)
        pairs.append((up_ref.at[at], up_hold.at[n], up_out.at[at]))
        pairs.append((down_ref.at[at], down_hold.at[n], down_out.at[at]))
    pairs.append((back_ref, back_hold, back_out))
    reads, copies = [], []
    for n, (source, hold, target) in enumerate(pairs):
        reads.append(pltpu.make_async_copy(source, hold, sems.at[0, n]))
        copies.append(pltpu.make_async_copy(hold, target, sems.at[1, n]))
    for copy in reads:
        copy.start()
    channels = up_ref.shape[0]
    for cb in range(channels // LANES):
        base, lanes = cb * 64, slice(cb * LANES, (cb + 1) * LANES)
        for i in range(ksize):
            row = base + i * ksize
            kernel_out[i, :, lanes] = small_ref[row : row + ksize, :]
        for n, out in enumerate((cbias_out, gain_out, lnb_out, downb_out, scale_out)):
            out[:, lanes] = small_ref[base + 49 + n : base + 50 + n, :]
        for fb in range(up_ref.shape[1] // channels):
            to = fb * channels + cb * LANES
            upb_out[:, to : to + LANES] = small_ref[base + 54 + fb : base + 55 + fb, :]
    for read, copy in zip(reads, copies):
        read.wait()
        copy.start()
    for copy in copies:
        copy.wait()


def shards(
    gx_count,
    gy_count,
    inputs,
    grad_out,
    conv_kernel,
    conv_bias,
    layer_norm_gain,
    layer_norm_bias,
    w_up,
    up_bias,
    w_down,
    down_bias,
    layer_scale,
):
    _, rows, columns, channels = inputs.shape
    ksize = conv_kernel.shape[0]
    pixels = rows * columns
    hidden_units = w_up.shape[1]
    line = lambda v: v.reshape(1, -1)
    vmem = pl.BlockSpec(memory_space=pltpu.VMEM)
    anywhere = pl.BlockSpec(memory_space=pl.ANY)
    high = rows + ksize - 1
    wide = -(-(columns + 2 * MARGIN) // 8) * 8
    limit = 60 * 1024 * 1024
    blocks = channels // LANES
    bits = (gx_count - 1).bit_length()
    small_rows = max(blocks * 64, 8 * gx_count * gy_count)
    chunks = 2 * hidden_units // channels
    others = gy_count - 1
    slots = 2 * (bits + others)
    left = channels // gx_count
    weight = jax.ShapeDtypeStruct((channels, hidden_units), F32)
    wide_rows = pltpu.VMEM((pixels, channels), F32)
    narrow_rows = pltpu.VMEM((pixels, channels), BF16)
    turned_rows = pltpu.VMEM((channels, pixels), BF16)
    whole = pltpu.VMEM((channels, hidden_units), F32)
    back, whole_up, whole_down, whole_small = pl.pallas_call(
        functools.partial(block_kernel, gx_count, gy_count, rows, columns, ksize),
        out_shape=(
            jax.ShapeDtypeStruct((pixels, channels), BF16),
            weight,
            weight,
            jax.ShapeDtypeStruct((small_rows, LANES), F32),
        ),
        in_specs=[vmem] * 11,
        out_specs=(vmem, anywhere, anywhere, vmem),
        scratch_shapes=[
            pltpu.VMEM((high, wide, channels), F32),
            pltpu.VMEM((high, wide, channels), F32),
            pltpu.VMEM((ksize, high, columns, LANES), F32),
            wide_rows,
            pltpu.VMEM((pixels, 1), F32),
            narrow_rows,
            turned_rows,
            narrow_rows,
            turned_rows,
            narrow_rows,
            narrow_rows,
            wide_rows,
            whole,
            whole,
            pltpu.VMEM((small_rows, LANES), F32),
            whole,
            whole,
            pltpu.VMEM((chunks, channels - left, channels), F32),
            pltpu.VMEM((chunks, others) + piece_shape(left, channels, gy_count)[1:], F32),
            pltpu.VMEM((small_rows, LANES), F32),
            pltpu.VMEM((others,) + piece_shape(small_rows // gx_count, LANES, gy_count)[1:], F32),
            pltpu.SemaphoreType.DMA((chunks + 1, slots)),
            pltpu.SemaphoreType.DMA((chunks + 1, slots)),
            pltpu.SemaphoreType.DMA((chunks,)),
        ],
        compiler_params=pltpu.CompilerParams(
            collective_id=0, has_side_effects=True, vmem_limit_bytes=limit
        ),
    )(
        inputs[0],
        grad_out.reshape(pixels, channels),
        conv_kernel,
        line(conv_bias),
        line(layer_norm_gain),
        line(layer_norm_bias),
        w_up,
        line(up_bias),
        w_down,
        line(down_bias),
        line(layer_scale),
    )

    parts = 4
    one = jax.ShapeDtypeStruct((1, channels), F32)
    results = pl.pallas_call(
        functools.partial(finish_kernel, ksize),
        out_shape=(
            jax.ShapeDtypeStruct((pixels, channels), BF16),
            jax.ShapeDtypeStruct(conv_kernel.shape, F32),
            one,
            one,
            one,
            weight,
            jax.ShapeDtypeStruct((1, hidden_units), F32),
            weight,
            one,
            one,
        ),
        in_specs=[anywhere, anywhere, anywhere, vmem],
        out_specs=(anywhere, vmem, vmem, vmem, vmem, anywhere, vmem, anywhere, vmem, vmem),
        scratch_shapes=[
            pltpu.VMEM((parts, channels // parts, hidden_units), F32),
            pltpu.VMEM((parts, channels // parts, hidden_units), F32),
            narrow_rows,
            pltpu.SemaphoreType.DMA((2, 2 * parts + 1)),
        ],
        compiler_params=pltpu.CompilerParams(vmem_limit_bytes=limit),
    )(whole_up, whole_down, back, whole_small)
    grad_inputs, g_kernel, cbias, ln_gain, lnb, g_up, upb, g_down, downb, scale = results
    flat = lambda v: v.reshape(-1)
    return (
        grad_inputs.reshape(inputs.shape),
        g_kernel,
        flat(cbias),
        flat(ln_gain),
        flat(lnb),
        g_up,
        flat(upb),
        g_down,
        flat(downb),
        flat(scale),
    )


def solution(mesh):
    image = P(("gx", "gy"), None, None, None)
    return jax.shard_map(
        functools.partial(shards, mesh.shape["gx"], mesh.shape["gy"]),
        mesh=mesh,
        in_specs=(image, image) + (P(),) * 9,
        out_specs=(image,) + (P(),) * 9,
        check_vma=False,
    )
```

```python
import functools

import jax
import jax.numpy as jnp
from jax import lax
from jax.experimental import pallas as pl
from jax.experimental.pallas import tpu as pltpu
from jax.sharding import PartitionSpec as P

MESH = pl.DeviceIdType.MESH
LANES = 128
MARGIN = 8
F32 = jnp.float32
BF16 = jnp.bfloat16


def fill_padded(pad, rows, columns, half, read):
    pad[...] = jnp.zeros_like(pad)

    def put(h, _):
        pad[h + half, MARGIN : MARGIN + columns, :] = read(h)
        return 0

    lax.fori_loop(0, rows, put, 0)


def fill_shifts(shifts, pad, lanes, ksize, columns):
    half = ksize // 2

    def put(r, _):
        for j in range(ksize):
            start = MARGIN - half + j
            shifts[j, r] = pad[r, start : start + columns, lanes]
        return 0

    lax.fori_loop(0, pad.shape[0], put, 0, unroll=2)


def add_rows(target, at, source, source_at, count, cols):
    tall = 32 if count % 32 == 0 else 8

    def one(r, _):
        to = pl.ds(pl.multiple_of(at + r * tall, 8), tall)
        here = pl.ds(pl.multiple_of(source_at + r * tall, 8), tall)
        target[to, :] += source[here, cols]
        return 0

    lax.fori_loop(0, count // tall, one, 0)


def piece_shape(size, width, parts):
    across = min(parts, width // LANES)
    return across, size * across // parts, width // across


def reduce_steps(gx_count, gy_count, order, acc, out, base, width, recv, zrecv, sends, recvs, pending):
    gi, zi = lax.axis_index("gx"), lax.axis_index("gy")
    fraction = 1.0 / (gx_count * gy_count)
    all_cols = slice(base, base + width)
    slot = [0]

    def send(src, dst, gx_to, gy_to):
        n = slot[0]
        slot[0] += 1
        copy = pltpu.make_async_remote_copy(
            src_ref=src,
            dst_ref=dst,
            send_sem=sends.at[n],
            recv_sem=recvs.at[n],
            device_id=(gx_to, gy_to),
            device_id_type=MESH,
        )
        copy.start()
        pending.append(copy)
        return copy

    def rows_at(at, n):
        return pl.ds(pl.multiple_of(at, 8), n)

    size, at, filled = acc.shape[0], 0, 0
    source, source_at, cols = acc, 0, all_cols
    for b in order:
        bit = (gi // 2**b) % 2
        other = gi + (1 - 2 * bit) * 2**b
        size //= 2
        give = source.at[rows_at(source_at + (1 - bit) * size, size), cols]
        copy = send(give, recv.at[filled : filled + size, :], other, zi)
        yield
        copy.wait_recv()
        add_rows(recv, filled, source, source_at + bit * size, size, cols)
        source, source_at, cols = recv, filled, slice(0, width)
        filled += size
        at = at + bit * size

    across, prows, pcols = piece_shape(size, width, gy_count)

    def piece(ref, z, top, left):
        there = rows_at(top + (z // across) * prows, prows)
        return ref.at[there, pl.ds(pl.multiple_of(left + (z % across) * pcols, LANES), pcols)]

    copies = []
    for d in range(1, gy_count):
        z = (zi + d) % gy_count
        copies.append(send(piece(recv, z, source_at, 0), zrecv.at[d - 1], gi, z))
    yield
    total = piece(recv, zi, source_at, 0)[...]
    for d in range(1, gy_count):
        copies[d - 1].wait_recv()
        total = total + zrecv[d - 1]
    done = piece(out, zi, at, base)
    done[...] = total * fraction
    copies = []
    for d in range(1, gy_count):
        z = (zi + d) % gy_count
        copies.append(send(done, done, gi, z))
    yield
    for copy in copies:
        copy.wait_recv()
    for b in reversed(order):
        bit = (gi // 2**b) % 2
        other = gi + (1 - 2 * bit) * 2**b
        mine = out.at[rows_at(at, size), all_cols]
        copy = send(mine, mine, other, zi)
        at = at - bit * size
        size *= 2
        yield
        copy.wait_recv()


def block_kernel(
    gx_count,
    gy_count,
    rows,
    columns,
    ksize,
    x_ref,
    up_ref,
    k_ref,
    cbias_ref,
    gain_ref,
    lnb_ref,
    wup_ref,
    upb_ref,
    wdown_ref,
    downb_ref,
    scale_ref,
    back_ref,
    up_out,
    down_out,
    small_out,
    pad_x,
    pad_g,
    shifts,
    xhat,
    inv,
    normed,
    normed_t,
    gb,
    gb_t,
    hid,
    gpre,
    gnormed,
    acc_up,
    acc_down,
    acc_small,
    full_up,
    full_down,
    recv,
    zrecv,
    recv_small,
    zrecv_small,
    sends,
    recvs,
    stores,
):
    pixels, channels = xhat.shape
    hidden_units = wup_ref.shape[1]
    half = ksize // 2
    block = channels
    blocks = channels // LANES
    bits = (gx_count - 1).bit_length()
    gi, zi = lax.axis_index("gx"), lax.axis_index("gy")
    barrier = pltpu.get_barrier_semaphore()
    for b in range(bits):
        bit = (gi // 2**b) % 2
        other = gi + (1 - 2 * bit) * 2**b
        pl.semaphore_signal(barrier, inc=1, device_id=(other, zi), device_id_type=MESH)
    for d in range(1, gy_count):
        z = (zi + d) % gy_count
        pl.semaphore_signal(barrier, inc=1, device_id=(gi, z), device_id_type=MESH)

    pending, live = [], []
    orders = ([0] + list(range(1, bits)), [0] + list(range(bits - 1, 0, -1)))

    def begin(n):
        acc, full, out = (
            (acc_down, full_down, down_out) if n % 2 == 0 else (acc_up, full_up, up_out)
        )
        cols = slice((n // 2) * block, (n // 2 + 1) * block)

        def run():
            yield from reduce_steps(
                gx_count, gy_count, orders[n % 2], acc, full, cols.start, block,
                recv.at[n], zrecv.at[n], sends.at[n], recvs.at[n], pending,
            )
            copy = pltpu.make_async_copy(full.at[:, cols], out.at[:, cols], stores.at[n])
            copy.start()
            finals.append(copy)

        return run()

    finals = []

    def advance(*fresh):
        for step in list(fresh) + live:
            try:
                next(step)
            except StopIteration:
                live.remove(step)
        live[:0] = fresh

    def put_small(row, value):
        for cb in range(blocks):
            at = cb * 64 + row
            acc_small[at : at + 1, :] = value[:, cb * LANES : (cb + 1) * LANES]

    fill_padded(pad_x, rows, columns, half, lambda h: x_ref[h].astype(F32))
    pad_g[...] = jnp.zeros_like(pad_g)
    acc_small[...] = jnp.zeros_like(acc_small)
    for cb in range(blocks):
        lanes = slice(cb * LANES, (cb + 1) * LANES)
        fill_shifts(shifts, pad_x, lanes, ksize, columns)

        def conv_row(h, _):
            total = jnp.zeros((columns, LANES), F32) + cbias_ref[:, lanes]
            for i in range(ksize):
                for j in range(ksize):
                    total = total + shifts[j, h + i] * k_ref[i, j : j + 1, lanes]
            xhat[pl.ds(pl.multiple_of(h * columns, 8), columns), lanes] = total
            return 0

        lax.fori_loop(0, rows, conv_row, 0)

    step = columns * 2
    gain = gain_ref[...]

    def norm_rows(b, carry):
        sum_up, sum_gb = carry
        at = pl.ds(pl.multiple_of(b * step, 16), step)
        mixed = xhat[at, :]
        removed = mixed - jnp.mean(mixed, axis=-1, keepdims=True)
        deviation = lax.rsqrt(jnp.mean(removed * removed, axis=-1, keepdims=True) + 1e-06)
        standard = removed * deviation
        xhat[at, :] = standard
        inv[at, :] = deviation
        normed[at, :] = (standard * gain + lnb_ref[...]).astype(BF16)
        upstream = up_ref[at, :].astype(F32)
        g_branch = (upstream * scale_ref[...]).astype(BF16)
        gb[at, :] = g_branch
        sum_up = sum_up + jnp.sum(upstream, axis=0, keepdims=True)
        sum_gb = sum_gb + jnp.sum(g_branch.astype(F32), axis=0, keepdims=True)
        return sum_up, sum_gb

    zero = jnp.zeros((1, channels), F32)
    sum_up, sum_gb = lax.fori_loop(0, pixels // step, norm_rows, (zero, zero))
    normed_t[...] = jnp.transpose(normed[...].astype(F32)).astype(BF16)
    gb_t[...] = jnp.transpose(gb[...].astype(F32)).astype(BF16)
    gnormed[...] = jnp.zeros_like(gnormed)
    put_small(52, sum_gb)
    tall = pixels // 3

    folded = jnp.zeros((channels, LANES), F32)
    for fb in range(hidden_units // block):
        cols = slice(fb * block, (fb + 1) * block)
        bias = upb_ref[:, cols]

        def mlp_rows(b, total):
            at = pl.ds(pl.multiple_of(b * tall, 16), tall)
            pre = jnp.dot(normed[at, :], wup_ref[:, cols], preferred_element_type=F32) + bias
            cdf = 0.5 * (1.0 + lax.erf(pre * 0.7071067811865476))
            hid[at, :] = (pre * cdf).astype(BF16)
            slope = cdf + pre * (jnp.exp(-0.5 * pre * pre) * 0.3989422804014327)
            g_hidden = jnp.dot(gb[at, :], wdown_ref[:, cols], preferred_element_type=F32)
            g = (g_hidden * slope).astype(BF16)
            gpre[at, :] = g
            gnormed[at, :] += lax.dot_general(
                g, wup_ref[:, cols], (((1,), (1,)), ((), ())), preferred_element_type=F32
            )
            return total + jnp.sum(g.astype(F32), axis=0, keepdims=True)

        total = lax.fori_loop(0, 3, mlp_rows, jnp.zeros((1, block), F32), unroll=3)
        put_small(54 + fb, total)
        acc_up[:, cols] = jnp.dot(normed_t[...], gpre[...], preferred_element_type=F32)
        gw = jnp.dot(gb_t[...], hid[...], preferred_element_type=F32)
        acc_down[:, cols] = gw
        if fb == 0:
            pl.semaphore_wait(barrier, bits + gy_count - 1)
        advance(begin(2 * fb), begin(2 * fb + 1))
        product = gw * wdown_ref[:, cols].astype(F32)
        for part in range(block // LANES):
            folded = folded + product[:, part * LANES : (part + 1) * LANES]

    scale_sum = jnp.sum(jnp.transpose(folded), axis=0, keepdims=True)
    put_small(53, scale_sum / scale_ref[...] + downb_ref[...] * sum_up)

    def back_rows(h, carry):
        s_gain, s_bias, s_conv = carry
        at = pl.ds(pl.multiple_of(h * columns, 16), columns)
        g, standard = gnormed[at, :], xhat[at, :]
        gx = g * gain
        mean_g = jnp.mean(gx, axis=-1, keepdims=True)
        mean_gx = jnp.mean(gx * standard, axis=-1, keepdims=True)
        gm = inv[at, :] * (gx - mean_g - standard * mean_gx)
        pad_g[h + half, MARGIN : MARGIN + columns, :] = gm
        return (
            s_gain + jnp.sum(g * standard, axis=0, keepdims=True),
            s_bias + jnp.sum(g, axis=0, keepdims=True),
            s_conv + jnp.sum(gm, axis=0, keepdims=True),
        )

    s_gain, s_bias, s_conv = lax.fori_loop(0, rows, back_rows, (zero, zero, zero), unroll=2)
    put_small(49, s_conv)
    put_small(50, s_gain)
    put_small(51, s_bias)
    advance()

    for cb in range(blocks):
        lanes = slice(cb * LANES, (cb + 1) * LANES)
        base = cb * 64
        fill_shifts(shifts, pad_x, lanes, ksize, columns)
        for j in range(ksize):

            def kernel_row(h, sums):
                g = pad_g[h + half, MARGIN : MARGIN + columns, lanes]
                new = []
                for i in range(ksize):
                    p = g * shifts[j, h + i]
                    part = p[0:8]
                    for w in range(8, columns, 8):
                        part = part + p[w : w + 8]
                    new.append(sums[i] + part)
                return tuple(new)

            zeros = tuple(jnp.zeros((8, LANES), F32) for _ in range(ksize))
            sums = lax.fori_loop(0, rows, kernel_row, zeros, unroll=4)
            for i in range(ksize):
                row = base + i * ksize + j
                acc_small[row : row + 1, :] = jnp.sum(sums[i], axis=0, keepdims=True)
        if cb == blocks - 1:
            advance(
                reduce_steps(
                    gx_count, gy_count, orders[0], acc_small, small_out, 0, LANES,
                    recv_small, zrecv_small, sends.at[sends.shape[0] - 1],
                    recvs.at[recvs.shape[0] - 1], pending,
                )
            )
        else:
            advance()

    for cb in range(blocks):
        lanes = slice(cb * LANES, (cb + 1) * LANES)
        fill_shifts(shifts, pad_g, lanes, ksize, columns)

        def back_row(h, _):
            at = pl.ds(pl.multiple_of(h * columns, 16), columns)
            total = up_ref[at, lanes].astype(F32)
            for i in range(ksize):
                for j in range(ksize):
                    total = total + (
                        shifts[ksize - 1 - j, h + (ksize - 1 - i)] * k_ref[i, j : j + 1, lanes]
                    )
            back_ref[at, lanes] = total.astype(BF16)
            return 0

        lax.fori_loop(0, rows // 2, back_row, 0)
        advance()
        lax.fori_loop(rows // 2, rows, back_row, 0)
        advance()

    while live:
        advance()
    for copy in pending:
        copy.wait_send()
    for copy in finals:
        copy.wait()


def finish_kernel(
    ksize,
    up_ref,
    down_ref,
    back_ref,
    small_ref,
    back_out,
    kernel_out,
    cbias_out,
    gain_out,
    lnb_out,
    up_out,
    upb_out,
    down_out,
    downb_out,
    scale_out,
    up_hold,
    down_hold,
    back_hold,
    sems,
):
    parts = up_hold.shape[0]
    tall = up_ref.shape[0] // parts
    pairs = []
    for n in range(parts):
        at = slice(n * tall, (n + 1) * tall)
        pairs.append((up_ref.at[at], up_hold.at[n], up_out.at[at]))
        pairs.append((down_ref.at[at], down_hold.at[n], down_out.at[at]))
    pairs.append((back_ref, back_hold, back_out))
    reads, copies = [], []
    for n, (source, hold, target) in enumerate(pairs):
        reads.append(pltpu.make_async_copy(source, hold, sems.at[0, n]))
        copies.append(pltpu.make_async_copy(hold, target, sems.at[1, n]))
    for copy in reads:
        copy.start()
    channels = up_ref.shape[0]
    for cb in range(channels // LANES):
        base, lanes = cb * 64, slice(cb * LANES, (cb + 1) * LANES)
        for i in range(ksize):
            row = base + i * ksize
            kernel_out[i, :, lanes] = small_ref[row : row + ksize, :]
        for n, out in enumerate((cbias_out, gain_out, lnb_out, downb_out, scale_out)):
            out[:, lanes] = small_ref[base + 49 + n : base + 50 + n, :]
        for fb in range(up_ref.shape[1] // channels):
            to = fb * channels + cb * LANES
            upb_out[:, to : to + LANES] = small_ref[base + 54 + fb : base + 55 + fb, :]
    for read, copy in zip(reads, copies):
        read.wait()
        copy.start()
    for copy in copies:
        copy.wait()


def shards(
    gx_count,
    gy_count,
    inputs,
    grad_out,
    conv_kernel,
    conv_bias,
    layer_norm_gain,
    layer_norm_bias,
    w_up,
    up_bias,
    w_down,
    down_bias,
    layer_scale,
):
    _, rows, columns, channels = inputs.shape
    ksize = conv_kernel.shape[0]
    pixels = rows * columns
    hidden_units = w_up.shape[1]
    line = lambda v: v.reshape(1, -1)
    vmem = pl.BlockSpec(memory_space=pltpu.VMEM)
    anywhere = pl.BlockSpec(memory_space=pl.ANY)
    high = rows + ksize - 1
    wide = -(-(columns + 2 * MARGIN) // 8) * 8
    limit = 60 * 1024 * 1024
    blocks = channels // LANES
    bits = (gx_count - 1).bit_length()
    small_rows = max(blocks * 64, 8 * gx_count * gy_count)
    chunks = 2 * hidden_units // channels
    others = gy_count - 1
    slots = 2 * (bits + others)
    left = channels // gx_count
    weight = jax.ShapeDtypeStruct((channels, hidden_units), F32)
    wide_rows = pltpu.VMEM((pixels, channels), F32)
    narrow_rows = pltpu.VMEM((pixels, channels), BF16)
    turned_rows = pltpu.VMEM((channels, pixels), BF16)
    whole = pltpu.VMEM((channels, hidden_units), F32)
    back, whole_up, whole_down, whole_small = pl.pallas_call(
        functools.partial(block_kernel, gx_count, gy_count, rows, columns, ksize),
        out_shape=(
            jax.ShapeDtypeStruct((pixels, channels), BF16),
            weight,
            weight,
            jax.ShapeDtypeStruct((small_rows, LANES), F32),
        ),
        in_specs=[vmem] * 11,
        out_specs=(vmem, anywhere, anywhere, vmem),
        scratch_shapes=[
            pltpu.VMEM((high, wide, channels), F32),
            pltpu.VMEM((high, wide, channels), F32),
            pltpu.VMEM((ksize, high, columns, LANES), F32),
            wide_rows,
            pltpu.VMEM((pixels, 1), F32),
            narrow_rows,
            turned_rows,
            narrow_rows,
            turned_rows,
            narrow_rows,
            narrow_rows,
            wide_rows,
            whole,
            whole,
            pltpu.VMEM((small_rows, LANES), F32),
            whole,
            whole,
            pltpu.VMEM((chunks, channels - left, channels), F32),
            pltpu.VMEM((chunks, others) + piece_shape(left, channels, gy_count)[1:], F32),
            pltpu.VMEM((small_rows, LANES), F32),
            pltpu.VMEM((others,) + piece_shape(small_rows // gx_count, LANES, gy_count)[1:], F32),
            pltpu.SemaphoreType.DMA((chunks + 1, slots)),
            pltpu.SemaphoreType.DMA((chunks + 1, slots)),
            pltpu.SemaphoreType.DMA((chunks,)),
        ],
        compiler_params=pltpu.CompilerParams(
            collective_id=0, has_side_effects=True, vmem_limit_bytes=limit
        ),
    )(
        inputs[0],
        grad_out.reshape(pixels, channels),
        conv_kernel,
        line(conv_bias),
        line(layer_norm_gain),
        line(layer_norm_bias),
        w_up,
        line(up_bias),
        w_down,
        line(down_bias),
        line(layer_scale),
    )

    parts = 4
    one = jax.ShapeDtypeStruct((1, channels), F32)
    results = pl.pallas_call(
        functools.partial(finish_kernel, ksize),
        out_shape=(
            jax.ShapeDtypeStruct((pixels, channels), BF16),
            jax.ShapeDtypeStruct(conv_kernel.shape, F32),
            one,
            one,
            one,
            weight,
            jax.ShapeDtypeStruct((1, hidden_units), F32),
            weight,
            one,
            one,
        ),
        in_specs=[anywhere, anywhere, anywhere, vmem],
        out_specs=(anywhere, vmem, vmem, vmem, vmem, anywhere, vmem, anywhere, vmem, vmem),
        scratch_shapes=[
            pltpu.VMEM((parts, channels // parts, hidden_units), F32),
            pltpu.VMEM((parts, channels // parts, hidden_units), F32),
            narrow_rows,
            pltpu.SemaphoreType.DMA((2, 2 * parts + 1)),
        ],
        compiler_params=pltpu.CompilerParams(vmem_limit_bytes=limit),
    )(whole_up, whole_down, back, whole_small)
    grad_inputs, g_kernel, cbias, ln_gain, lnb, g_up, upb, g_down, downb, scale = results
    flat = lambda v: v.reshape(-1)
    return (
        grad_inputs.reshape(inputs.shape),
        g_kernel,
        flat(cbias),
        flat(ln_gain),
        flat(lnb),
        g_up,
        flat(upb),
        g_down,
        flat(downb),
        flat(scale),
    )


def solution(mesh):
    image = P(("gx", "gy"), None, None, None)
    return jax.shard_map(
        functools.partial(shards, mesh.shape["gx"], mesh.shape["gy"]),
        mesh=mesh,
        in_specs=(image, image) + (P(),) * 9,
        out_specs=(image,) + (P(),) * 9,
        check_vma=False,
    )
```
